32 devices in a mesh: experts: 8 (over z, y), context: 4 (over x, core).
Axes of the slice: x: 2, y: 2, z: 4, core: 2. Of those that a mesh axis runs over, the one named last changes fastest.
Arguments:
- block_input: bfloat16 [8, 512, 768], P('experts', 'context'), may hold values from -6 to 6
- first_gain: float32 [768], replicated, may hold values from 0.5 to 1.5
- second_gain: float32 [768], replicated, may hold values from 0.5 to 1.5
- qkv_weight: bfloat16 [768, 2304], replicated, may hold values from -0.21875 to 0.21875
- out_weight: bfloat16 [768, 768], replicated, may hold values from -0.21875 to 0.21875
- rel_table: float32 [32, 12], replicated, may hold values from -2 to 2
- bucket_ids: int32 [512, 512], P('context'), may hold values from 0 to 31
- expert_route: int32 [8, 512], P('experts', 'context'), may hold values from 0 to 15, as said below
- expert_slot: int32 [8, 512], P('experts', 'context'), may hold values from 0 to 9, as said below
- gate_value: float32 [8, 512], P('experts', 'context'), may hold values from 0.5 to 1.5
- expert_in: bfloat16 [16, 768, 3072], P('experts', None, 'context'), may hold values from -0.21875 to 0.21875
- expert_down: bfloat16 [16, 3072, 768], P('experts', 'context'), may hold values from -0.15625 to 0.15625
- upstream: bfloat16 [8, 512, 768], P('experts', 'context'), may hold values from -6 to 6
Outputs:
- block_output: bfloat16 [8, 512, 768], P('experts', 'context')
- input_grad: float32 [8, 512, 768], P('experts', 'context')
- qkv_grad: float32 [768, 2304], P('experts')
- proj_grad: float32 [768, 768], P('experts')
- first_grad: float32 [768], P('experts')
- second_grad: float32 [768], P('experts')
- table_grad: float32 [32, 12], P('experts')
- inner_grad: float32 [16, 768, 3072], P('experts', None, 'context')
- down_grad: float32 [16, 3072, 768], P('experts', 'context')
The draws below stay inside these ranges and needn't reach their ends.
Inputs may be any that keep to these rules, and one draw needn't show every extreme that they name: `expert_route`: within each aligned block of 128 consecutive tokens of a sequence no expert is named by more than 10 tokens; one expert, the same in every block, is named by exactly 10 tokens in every block, and so is a second one drawn for each block (in some blocks the two are the same expert); the other tokens of a block spread over the remaining slots. Within each aligned block of 128 tokens the pairs of expert_route and expert_slot are distinct.
All inputs are finite; a program needn't handle non-finite values.
Results may differ from the reference program's by a relative error of at most 0.033.
Values may be sent and summed in bfloat16 or wider, within the bound.
A program may use at most 192 MiB of HBM per device.

```python
import math
import jax
import jax.numpy as jnp
from jax import lax

D = 768
HEADS = 12
HEAD = 64
FF = 3072
BUCKETS = 32
TOK_DEV = 128
SEQS = 8
LEN = 512
EXPERTS = 16
CAP = 10


def route_plan(key):
    block_count = SEQS * (LEN // TOK_DEV)
    slot_total = EXPERTS * CAP
    favored = jax.random.randint(jax.random.fold_in(key, 1), (), 0, EXPERTS)
    owners = jnp.arange(slot_total, dtype=jnp.int32) // CAP

    def one_block(block_key):
        second = jax.random.randint(jax.random.fold_in(block_key, 2), (), 0, EXPERTS)
        priority = jax.random.permutation(jax.random.fold_in(block_key, 3), slot_total).astype(jnp.int32)
        boosted = ((owners == favored) | (owners == second)).astype(jnp.int32)
        ranked = priority + slot_total * boosted
        chosen = jnp.argsort(-ranked)[:TOK_DEV]
        placed = jax.random.permutation(jax.random.fold_in(block_key, 4), chosen).astype(jnp.int32)
        return (placed // CAP, placed % CAP)
    block_keys = jax.random.split(jax.random.fold_in(key, 5), block_count)
    routes, slot_ids = jax.vmap(one_block)(block_keys)
    return (routes.reshape(SEQS, LEN).astype(jnp.int32), slot_ids.reshape(SEQS, LEN).astype(jnp.int32))


def draw_expert_route(key, part):
    return route_plan(jax.random.fold_in(key, 17))[0]


def draw_expert_slot(key, part):
    return route_plan(jax.random.fold_in(key, 17))[1]


def place_ends(array, key, least, high):
    shape = array.shape
    place = [jax.random.randint(jax.random.fold_in(key, axis), (), 0, shape[axis]) for axis in range(len(shape))]
    array = array.at[tuple(place)].set(least)
    longest = shape.index(max(shape))
    place[longest] = (place[longest] + 1) % shape[longest]
    return array.at[tuple(place)].set(high)


def spiked(drawn, key, source, target, parts, factor):
    owner, partner = [(jnp.arange(drawn.shape[axis_at]) // (drawn.shape[axis_at] // parts)).reshape([-1 if axis == axis_at else 1 for axis in range(drawn.ndim)]) for axis_at in (source, target)]
    chosen = jax.random.permutation(key, parts)[partner]
    strong = (owner == chosen) | (owner == (partner + parts // 2) % parts)
    return jnp.where(strong, factor * drawn, drawn)


def levels(key, shape, shards, smallest, largest):
    def one(axis_at, parts):
        heights = jax.random.uniform(jax.random.fold_in(jax.random.fold_in(key, 6), axis_at), (parts,), jnp.float32, smallest / len(shards), largest / len(shards))
        return jnp.repeat(jnp.exp(heights), shape[axis_at] // parts).reshape((-1,) + (1,) * (len(shape) - axis_at - 1))

    level = one(*shards[0])
    for cut in shards[1:]:
        level = level * one(*cut)
    return level


def gaussian(key, shape, spread, bound, cuts=(), kind=jnp.bfloat16):
    values = spread * jax.random.normal(key, shape, jnp.float32)
    if cuts:
        values = values * levels(key, shape, cuts, -0.22, 0.18)
    return jnp.clip(values, -bound, bound).astype(kind)


def bell_draw_with(rng, shape, scale, limit, cuts, heavy, held_as=jnp.bfloat16):
    values = scale * jax.random.normal(rng, shape, jnp.float32)
    if cuts:
        values = values * levels(rng, shape, cuts, -0.22, 0.18)
    return jnp.clip(spiked(values, jax.random.fold_in(rng, 3), *heavy), -limit, limit).astype(held_as)


def setup_inputs(seed: int = 0) -> dict:
    splits = jax.random.split(jax.random.key(seed), 14)
    return {
        "block_input": bell_draw_with(splits[0], (SEQS, LEN, D), 1.0, 6.0, ((0, 8), (1, 4)), (0, 2, 8, 2.0)),
        "first_gain": jnp.clip(1.0 + 0.1 * jax.random.normal(splits[1], (D,), jnp.float32), 0.5, 1.5),
        "second_gain": jnp.clip(1.0 + 0.1 * jax.random.normal(splits[2], (D,), jnp.float32), 0.5, 1.5),
        "qkv_weight": gaussian(splits[3], (D, 3 * D), D ** -0.5, 0.21875),
        "out_weight": gaussian(splits[4], (D, D), D ** -0.5, 0.21875),
        "rel_table": jnp.clip(jax.random.uniform(splits[5], (BUCKETS, HEADS), jnp.float32, -2.0, 2.0), -2.0, 2.0),
        "bucket_ids": place_ends(jax.random.randint(splits[6], (LEN, LEN), 0, BUCKETS), jax.random.fold_in(splits[6], 1), 0, BUCKETS - 1).astype(jnp.int32),
        "expert_route": draw_expert_route(jax.random.fold_in(splits[13], 71), 0),
        "expert_slot": draw_expert_slot(jax.random.fold_in(splits[13], 71), 0),
        "gate_value": jnp.clip(0.5 + 1.0 * jax.random.uniform(splits[9], (SEQS, LEN), jnp.float32) ** levels(splits[9], (SEQS, LEN), ((0, 8), (1, 4)), -0.2, 0.2), 0.5, 1.5),
        "expert_in": gaussian(splits[10], (EXPERTS, D, FF), D ** -0.5, 0.21875, ((0, 8), (2, 4))),
        "expert_down": gaussian(splits[11], (EXPERTS, FF, D), (FF // 2) ** -0.5, 0.15625, ((0, 8), (1, 4))),
        "upstream": gaussian(splits[12], (SEQS, LEN, D), 1.0, 6.0, ((0, 8), (1, 4))),
    }


norm_eps = 1e-06

def rms_scale(values, gain):
    factor = lax.rsqrt(lax.optimization_barrier(jnp.mean(values * values, axis=-1, keepdims=True)) + norm_eps)
    return values * factor * gain

def make_scores(queries, keys_all, bucket_rows, table_heads):
    score_scale = 1.0 / math.sqrt(HEAD)
    q_heads = queries.astype(jnp.float32).reshape(LEN, HEADS, HEAD)
    k_heads = keys_all.astype(jnp.float32).reshape(LEN, HEADS, HEAD)
    dots = jnp.einsum('qhd,khd->hqk', q_heads, k_heads, precision=lax.Precision.HIGHEST)
    return dots * score_scale + jnp.take(table_heads, bucket_rows, axis=1)

def attend_forward(queries, keys_all, values_all, bucket_rows, table_heads):
    scores = make_scores(queries, keys_all, bucket_rows, table_heads)
    log_total = jax.nn.logsumexp(scores, axis=-1)
    weights = jnp.exp(scores - log_total[:, :, None])
    v_heads = values_all.astype(jnp.float32).reshape(LEN, HEADS, HEAD)
    attended = jnp.einsum('hqk,khd->qhd', weights, v_heads, precision=lax.Precision.HIGHEST)
    return (attended.reshape(LEN, D).astype(jnp.bfloat16), log_total)

def attend_backward(queries, keys_all, values_all, bucket_rows, table_heads, attended, log_total, d_att):
    score_scale = 1.0 / math.sqrt(HEAD)
    scores = make_scores(queries, keys_all, bucket_rows, table_heads)
    probs = jnp.exp(scores - log_total[:, :, None])
    weights_wide = lax.optimization_barrier(probs.astype(jnp.bfloat16)).astype(jnp.float32)
    q_heads = queries.astype(jnp.float32).reshape(LEN, HEADS, HEAD)
    k_heads = keys_all.astype(jnp.float32).reshape(LEN, HEADS, HEAD)
    v_heads = values_all.astype(jnp.float32).reshape(LEN, HEADS, HEAD)
    grad_heads = d_att.astype(jnp.float32).reshape(LEN, HEADS, HEAD)
    att_heads = attended.astype(jnp.float32).reshape(LEN, HEADS, HEAD)
    delta = lax.optimization_barrier(jnp.sum(grad_heads * att_heads, axis=-1)).T
    d_probs = jnp.einsum('qhd,khd->hqk', grad_heads, v_heads, precision=lax.Precision.HIGHEST)
    d_scores = probs * (d_probs - delta[:, :, None])
    scores_round = lax.optimization_barrier(d_scores.astype(jnp.bfloat16)).astype(jnp.float32)
    d_queries = jnp.einsum('hqk,khd->qhd', scores_round, k_heads, precision=lax.Precision.HIGHEST) * score_scale
    d_keys = jnp.einsum('hqk,qhd->khd', scores_round, q_heads, precision=lax.Precision.HIGHEST) * score_scale
    d_values = jnp.einsum('hqk,qhd->khd', weights_wide, grad_heads, precision=lax.Precision.HIGHEST)
    flat_scores = jnp.transpose(d_scores, (1, 2, 0)).reshape(LEN * LEN, HEADS)
    table_part = jax.ops.segment_sum(flat_scores, bucket_rows.reshape(-1), num_segments=BUCKETS)
    stacked = jnp.concatenate([d_queries.reshape(LEN, D), d_keys.reshape(LEN, D), d_values.reshape(LEN, D)], axis=1)
    return (stacked, table_part)

def reference(block_input, first_gain, second_gain, qkv_weight, out_weight, rel_table, bucket_ids, expert_route, expert_slot, gate_value, expert_in, expert_down, upstream):
    features = block_input.astype(jnp.float32)
    normed = rms_scale(features, first_gain).astype(jnp.bfloat16)
    qkv_all = jnp.dot(normed.reshape(-1, D), qkv_weight, preferred_element_type=jnp.float32).astype(jnp.bfloat16).reshape(SEQS, LEN, 3 * D)
    table_heads = rel_table.T

    def forward_one(qkv_seq):
        return attend_forward(qkv_seq[:, :D], qkv_seq[:, D:2 * D], qkv_seq[:, 2 * D:], bucket_ids, table_heads)
    attended, log_total = lax.map(forward_one, qkv_all)
    middle = features + jnp.dot(attended.reshape(-1, D), out_weight, preferred_element_type=jnp.float32).reshape(SEQS, LEN, D)
    second_normed = rms_scale(middle, second_gain)
    blocks = SEQS * (LEN // TOK_DEV)
    block_rows = second_normed.reshape(blocks, TOK_DEV, D)
    route_rows = expert_route.reshape(blocks, TOK_DEV)
    slot_rows = expert_slot.reshape(blocks, TOK_DEV)
    block_index = jnp.broadcast_to(jnp.arange(blocks, dtype=jnp.int32)[:, None], (blocks, TOK_DEV))
    buffer = jnp.zeros((EXPERTS, blocks, CAP, D), jnp.float32).at[route_rows, block_index, slot_rows].set(block_rows)

    def expert_forward(operands):
        rows_in, weight_in, weight_down = operands
        flat_rows = rows_in.reshape(blocks * CAP, D)
        pre_act = jnp.dot(flat_rows, weight_in.astype(jnp.float32), precision=lax.Precision.HIGHEST)
        hidden = jnp.maximum(pre_act, 0.0).astype(jnp.bfloat16)
        return jnp.dot(hidden, weight_down, preferred_element_type=jnp.float32).astype(jnp.bfloat16).reshape(blocks, CAP, D)
    expert_out = lax.map(expert_forward, (buffer, expert_in, expert_down))
    picked = expert_out[route_rows, block_index, slot_rows].reshape(SEQS, LEN, D).astype(jnp.float32)
    block_output = (middle + gate_value[:, :, None] * picked).astype(jnp.bfloat16)
    grad_top = upstream.astype(jnp.float32)
    scaled = (gate_value[:, :, None] * grad_top).astype(jnp.bfloat16).reshape(blocks, TOK_DEV, D)
    back_out = jnp.zeros((EXPERTS, blocks, CAP, D), jnp.bfloat16).at[route_rows, block_index, slot_rows].set(scaled)

    def expert_backward(operands):
        rows_in, grads_out, weight_in, weight_down = operands
        flat_rows = rows_in.reshape(blocks * CAP, D)
        grad_flat = grads_out.reshape(blocks * CAP, D)
        pre_act = jnp.dot(flat_rows, weight_in.astype(jnp.float32), precision=lax.Precision.HIGHEST)
        hidden = jnp.maximum(pre_act, 0.0).astype(jnp.bfloat16)
        down_part = jnp.dot(hidden.T, grad_flat, preferred_element_type=jnp.float32)
        hidden_grad = jnp.dot(grad_flat, weight_down.T, preferred_element_type=jnp.float32)
        pre_grad = jnp.where(pre_act > 0.0, hidden_grad, 0.0).astype(jnp.bfloat16)
        inner_part = jnp.dot(flat_rows.T, pre_grad.astype(jnp.float32), precision=lax.Precision.HIGHEST)
        back_in = jnp.dot(pre_grad, weight_in.T, preferred_element_type=jnp.float32).astype(jnp.bfloat16)
        return (inner_part, down_part, back_in.reshape(blocks, CAP, D))
    inner_grad, down_grad, back_in = lax.map(expert_backward, (buffer, back_out, expert_in, expert_down))
    d_second = back_in[route_rows, block_index, slot_rows].reshape(SEQS, LEN, D).astype(jnp.float32)
    _, second_pull = jax.vjp(rms_scale, middle, second_gain)
    d_middle_norm, second_grad = second_pull(d_second)
    d_middle = grad_top + d_middle_norm
    d_middle_b = d_middle.astype(jnp.bfloat16)
    proj_grad = jnp.dot(attended.reshape(-1, D).T, d_middle_b.reshape(-1, D), preferred_element_type=jnp.float32)
    d_att = jnp.dot(d_middle_b.reshape(-1, D), out_weight.T, preferred_element_type=jnp.float32).astype(jnp.bfloat16).reshape(SEQS, LEN, D)

    def backward_one(operands):
        qkv_seq, att_seq, lse_seq, grad_seq = operands
        return attend_backward(qkv_seq[:, :D], qkv_seq[:, D:2 * D], qkv_seq[:, 2 * D:], bucket_ids, table_heads, att_seq, lse_seq, grad_seq)
    d_qkv_wide, table_parts = lax.map(backward_one, (qkv_all, attended, log_total, d_att))
    table_grad = lax.optimization_barrier(jnp.sum(table_parts, axis=0))
    d_qkv = d_qkv_wide.astype(jnp.bfloat16).reshape(-1, 3 * D)
    qkv_grad = jnp.dot(normed.reshape(-1, D).T, d_qkv, preferred_element_type=jnp.float32)
    d_first = jnp.dot(d_qkv, qkv_weight.T, preferred_element_type=jnp.float32).reshape(SEQS, LEN, D)
    _, first_pull = jax.vjp(rms_scale, features, first_gain)
    d_input_norm, first_grad = first_pull(d_first)
    input_grad = d_middle + d_input_norm
    return (block_output, input_grad, qkv_grad, proj_grad, first_grad, second_grad, table_grad, inner_grad, down_grad)
```

```python
import functools
import math

import jax
import jax.numpy as jnp
from jax import lax
from jax.experimental import pallas as pl
from jax.experimental.pallas import tpu as pltpu
from jax.sharding import PartitionSpec as P

norm_eps = 1e-06
f32 = jnp.float32
bf16 = jnp.bfloat16
NT = (((1,), (1,)), ((), ()))
TN = (((0,), (0,)), ((), ()))
VMEM_BYTES = 48 * 1024 * 1024


def rms_scale(values, gain):
    factor = lax.rsqrt(jnp.mean(values * values, axis=-1, keepdims=True) + norm_eps)
    return values * factor * gain


def dot(a, b, dims=(((1,), (0,)), ((), ()))):
    return lax.dot_general(a, b, dims, preferred_element_type=f32)


def lane_lookup(row, index):
    source = jnp.broadcast_to(row, index.shape)
    numbers = lax.GatherDimensionNumbers(
        offset_dims=(),
        collapsed_slice_dims=(1,),
        start_index_map=(1,),
        operand_batching_dims=(0,),
        start_indices_batching_dims=(0,),
    )
    return lax.gather(
        source,
        index[..., None],
        numbers,
        slice_sizes=(1, 1),
        mode=lax.GatherScatterMode.PROMISE_IN_BOUNDS,
    )


def forward_kernel(scale, step, q_ref, k_ref, v_ref, table_ref, ids_ref, att_ref, prob_ref):
    total = ids_ref.shape[0]
    keys = k_ref[0]
    values = v_ref[0]
    row = table_ref[0]

    @pl.loop(0, total // step)
    def _(index):
        rows = pl.ds(pl.multiple_of(index * step, step), step)
        scores = dot(q_ref[0, rows, :], keys, NT) * scale
        ids = ids_ref[rows, :].astype(f32).astype(jnp.int32)
        bias = [lane_lookup(row, ids[:, at : at + 128]) for at in range(0, total, 128)]
        scores = scores + jnp.concatenate(bias, axis=1)
        expons = jnp.exp(scores - jnp.max(scores, axis=1, keepdims=True))
        probs = (expons / jnp.sum(expons, axis=1, keepdims=True)).astype(bf16)
        prob_ref[0, rows, :] = probs
        att_ref[0, rows, :] = dot(probs, values).astype(bf16)


def backward_kernel(
    scale, step, q_ref, k_ref, v_ref, att_ref, grad_ref, prob_ref, dq_ref, dk_ref, dv_ref, ds_ref,
    dk_sum, dv_sum,
):
    total = q_ref.shape[1]
    keys = k_ref[0]
    values = v_ref[0]
    dk_sum[...] = jnp.zeros_like(dk_sum)
    dv_sum[...] = jnp.zeros_like(dv_sum)

    @pl.loop(0, total // step)
    def _(index):
        rows = pl.ds(pl.multiple_of(index * step, step), step)
        grad = grad_ref[0, rows, :]
        probs = prob_ref[0, rows, :]
        delta = jnp.sum(
            grad.astype(f32) * att_ref[0, rows, :].astype(f32), axis=1, keepdims=True
        )
        d_scores = (probs.astype(f32) * (dot(grad, values, NT) - delta)).astype(bf16)
        ds_ref[0, rows, :] = d_scores
        dq_ref[0, rows, :] = (dot(d_scores, keys) * scale).astype(bf16)
        dk_sum[...] += dot(d_scores, q_ref[0, rows, :], TN)
        dv_sum[...] += dot(probs, grad, TN)

    dk_ref[0] = (dk_sum[...] * scale).astype(bf16)
    dv_ref[0] = dv_sum[...].astype(bf16)


def table_kernel(buckets, ds_ref, ids_ref, out_ref):
    total = ids_ref.shape[0]
    width = ids_ref.shape[1]
    group = 64

    def one_bucket(bucket, _):
        wanted = bucket.astype(f32).astype(bf16)

        def one_group(index, acc):
            rows = pl.ds(pl.multiple_of(index * group, group), group)
            picked = jnp.where(ids_ref[rows, :] == wanted, ds_ref[0, rows, :], jnp.zeros((), bf16))
            part = picked[0:16] + picked[16:32]
            for at in range(32, group, 16):
                part = part + picked[at : at + 16]
            return acc + part.astype(f32)

        acc = lax.fori_loop(0, total // group, one_group, jnp.zeros((16, width), f32), unroll=True)
        out_ref[0, pl.ds(bucket, 1), :] = jnp.sum(acc, axis=0, keepdims=True)
        return 0

    lax.fori_loop(0, buckets, one_bucket, 0)


def head_spec(rows, columns):
    return pl.BlockSpec((1, rows, columns), lambda h: (h, 0, 0))


def attend(q, k, v, table, ids):
    heads, total, size = q.shape
    scale = 1.0 / math.sqrt(size)
    return pl.pallas_call(
        functools.partial(forward_kernel, scale, 128),
        grid=(heads,),
        in_specs=[head_spec(total, size)] * 3
        + [head_spec(1, 128), pl.BlockSpec((total, total), lambda h: (0, 0))],
        out_specs=[head_spec(total, size), head_spec(total, total)],
        out_shape=[
            jax.ShapeDtypeStruct((heads, total, size), bf16),
            jax.ShapeDtypeStruct((heads, total, total), bf16),
        ],
        cost_estimate=pl.CostEstimate(
            flops=4 * heads * total * total * size,
            bytes_accessed=4 * heads * total * total,
            transcendentals=heads * total * total,
        ),
        compiler_params=pltpu.CompilerParams(vmem_limit_bytes=VMEM_BYTES),
        name="attend",
    )(q, k, v, table, ids)


def attend_back(q, k, v, att, grad, probs):
    heads, total, size = q.shape
    scale = 1.0 / math.sqrt(size)
    small = jax.ShapeDtypeStruct((heads, total, size), bf16)
    return pl.pallas_call(
        functools.partial(backward_kernel, scale, 128),
        grid=(heads,),
        in_specs=[head_spec(total, size)] * 5 + [head_spec(total, total)],
        out_specs=[head_spec(total, size)] * 3 + [head_spec(total, total)],
        out_shape=[small] * 3 + [jax.ShapeDtypeStruct((heads, total, total), bf16)],
        scratch_shapes=[pltpu.VMEM((total, size), f32)] * 2,
        cost_estimate=pl.CostEstimate(
            flops=8 * heads * total * total * size,
            bytes_accessed=8 * heads * total * total,
            transcendentals=0,
        ),
        compiler_params=pltpu.CompilerParams(vmem_limit_bytes=VMEM_BYTES),
        name="attend_back",
    )(q, k, v, att, grad, probs)


def table_sums(d_scores, ids, buckets):
    heads, total, _ = d_scores.shape
    sums = pl.pallas_call(
        functools.partial(table_kernel, buckets),
        grid=(heads,),
        in_specs=[head_spec(total, total), pl.BlockSpec((total, total), lambda h: (0, 0))],
        out_specs=head_spec(buckets, total),
        out_shape=jax.ShapeDtypeStruct((heads, buckets, total), f32),
        cost_estimate=pl.CostEstimate(
            flops=64 * heads * total * total,
            bytes_accessed=4 * heads * total * total,
            transcendentals=0,
        ),
        compiler_params=pltpu.CompilerParams(vmem_limit_bytes=VMEM_BYTES),
        name="table_sums",
    )(d_scores, ids)
    return jnp.sum(sums, axis=2)


def body(
    block_input,
    first_gain,
    second_gain,
    qkv_weight,
    out_weight,
    rel_table,
    bucket_ids,
    expert_route,
    expert_slot,
    gate_value,
    expert_in,
    expert_down,
    upstream,
):
    ranks = lax.axis_size("context")
    me = lax.axis_index("context")
    expert_ranks = lax.axis_size("experts")
    local_rows, width = block_input.shape[1:]
    buckets, heads = rel_table.shape
    size = width // heads
    total = bucket_ids.shape[1]
    group = -(-heads // ranks)
    spare = group * ranks - heads
    share = group * size
    columns = width // ranks
    experts_local = expert_in.shape[0]
    experts_total = experts_local * expert_ranks
    capacity = max(4, 4 * local_rows // (3 * experts_total))
    slots = experts_total * capacity
    local_slots = experts_local * capacity

    features = block_input[0].astype(f32)
    gates = gate_value[0][:, None]
    grad_top = upstream[0].astype(f32)
    place = expert_route[0] * capacity + expert_slot[0]
    chosen = (place[None, :] == jnp.arange(slots, dtype=jnp.int32)[:, None]).astype(bf16)

    def send_rows(rows):
        spread = dot(chosen, rows).astype(bf16).reshape(expert_ranks, local_slots, -1)
        arrived = lax.all_to_all(spread, "experts", split_axis=0, concat_axis=0, tiled=True)
        return lax.all_gather(arrived, "context", axis=0, tiled=True)

    shared = lax.all_gather(
        jnp.concatenate([block_input[0], bucket_ids.astype(bf16)], axis=1),
        "context",
        axis=0,
        tiled=True,
    )
    all_features = shared[:, :width].astype(f32)
    ids = shared[:, width:]
    grad_rows = send_rows((gates * grad_top).astype(bf16))
    normed = rms_scale(all_features, first_gain).astype(bf16)
    weight = jnp.pad(
        qkv_weight.reshape(width, 3, heads * size), ((0, 0), (0, 0), (0, spare * size))
    )
    my_weight = lax.dynamic_slice_in_dim(weight, me * share, share, 2).reshape(width, 3 * share)
    qkv = (
        dot(normed, my_weight)
        .astype(bf16)
        .reshape(total, 3, group, size)
        .transpose(1, 2, 0, 3)
    )
    q, k, v = qkv[0], qkv[1], qkv[2]
    table = jnp.pad(rel_table.T, ((0, spare), (0, 128 - buckets)))
    my_table = lax.dynamic_slice_in_dim(table, me * group, group, 0)[:, None, :]
    att, probs = attend(q, k, v, my_table, ids)
    all_att = lax.all_gather(
        att.transpose(1, 0, 2).reshape(total, share), "context", axis=0, tiled=False
    )
    all_att = all_att.transpose(1, 0, 2).reshape(total, ranks * share)[:, :width]
    attended = lax.dynamic_slice_in_dim(all_att, me * local_rows, local_rows, 0)
    middle = features + dot(attended, out_weight)
    second_normed = rms_scale(middle, second_gain)

    high_wide = lax.reduce_precision(second_normed, 8, 7)
    high = high_wide.astype(bf16)
    low = (second_normed - high_wide).astype(bf16)
    gathered = send_rows(jnp.concatenate([high, low], axis=1))

    def by_expert(rows):
        rows = rows.reshape(ranks * expert_ranks, experts_local, capacity, -1)
        return rows.transpose(1, 0, 2, 3).reshape(
            experts_local, ranks * expert_ranks * capacity, -1
        )

    def by_block(rows):
        rows = rows.reshape(experts_local, ranks, expert_ranks, capacity, -1)
        return rows.transpose(1, 2, 0, 3, 4).reshape(ranks, expert_ranks, local_slots, -1)

    wide = by_expert(gathered)
    grads = by_expert(grad_rows)
    high_rows, low_rows = wide[:, :, :width], wide[:, :, width:]
    batched = functools.partial(jnp.einsum, preferred_element_type=f32)
    pre_act = batched("xnd,xdf->xnf", high_rows, expert_in) + batched(
        "xnd,xdf->xnf", low_rows, expert_in
    )
    hidden = jnp.maximum(pre_act, 0.0).astype(bf16)
    hidden_grad = batched("xnd,xfd->xnf", grads, expert_down)
    pre_grad = jnp.where(pre_act > 0.0, hidden_grad, 0.0).astype(bf16)
    forward_out = batched("xnf,xfd->xnd", hidden, expert_down).astype(bf16)
    back_in = batched("xnf,xdf->xnd", pre_grad, expert_in).astype(bf16)
    partial = by_block(jnp.concatenate([forward_out, back_in], axis=2))
    pieces = lax.all_to_all(partial, "context", split_axis=0, concat_axis=0, tiled=True)
    summed = jnp.sum(pieces.astype(f32), axis=0).astype(bf16)
    returned = lax.all_to_all(summed, "experts", split_axis=0, concat_axis=0, tiled=True)
    picked = dot(chosen, returned.reshape(slots, 2 * width), TN)
    inner_grad = batched("xnd,xnf->xdf", high_rows, pre_grad)
    down_grad = batched("xnf,xnd->xfd", hidden, grads)
    block_output = (middle + gates * picked[:, :width]).astype(bf16)[None]

    _, second_pull = jax.vjp(rms_scale, middle, second_gain)
    d_middle_norm, second_part = second_pull(picked[:, width:])
    d_middle = grad_top + d_middle_norm
    all_d_middle = lax.all_gather(d_middle.astype(bf16), "context", axis=0, tiled=True)

    out_rows = jnp.pad(out_weight, ((0, spare * size), (0, 0)))
    my_out = lax.dynamic_slice_in_dim(out_rows, me * share, share, 0)
    d_att = (
        dot(all_d_middle, my_out, NT).astype(bf16).reshape(total, group, size).transpose(1, 0, 2)
    )
    dq, dk, dv, d_scores = attend_back(q, k, v, att, d_att, probs)
    d_qkv = jnp.stack([dq, dk, dv]).transpose(2, 0, 1, 3).reshape(total, 3 * share)
    own = lax.all_to_all(
        d_qkv.reshape(ranks, local_rows, 3 * share),
        "context",
        split_axis=0,
        concat_axis=0,
        tiled=True,
    )
    own = own.reshape(ranks, local_rows, 3, share).transpose(1, 2, 0, 3)
    own = own.reshape(local_rows, 3, ranks * share)[:, :, :width].reshape(local_rows, 3 * width)
    d_first = dot(own, qkv_weight, NT)
    _, first_pull = jax.vjp(rms_scale, features, first_gain)
    d_input_norm, first_part = first_pull(d_first)
    input_grad = (d_middle + d_input_norm)[None]

    my_d_middle = lax.dynamic_slice_in_dim(all_d_middle, me * columns, columns, 1)
    qkv_part = dot(normed, d_qkv, TN)
    proj_part = dot(all_att, my_d_middle, TN)
    table_part = table_sums(d_scores, ids, buckets).T
    wide_part = jnp.concatenate([qkv_part, proj_part], axis=1).astype(bf16)
    grad_width = 3 * share + columns
    rows_out = width // expert_ranks
    table_out = buckets // expert_ranks
    small = jnp.concatenate(
        [
            first_part.reshape(expert_ranks, rows_out),
            second_part.reshape(expert_ranks, rows_out),
            table_part.reshape(expert_ranks, table_out * group),
        ],
        axis=1,
    ).astype(bf16)
    small = jnp.pad(small, ((0, 0), (0, grad_width - small.shape[1])))
    wide_part = jnp.concatenate(
        [wide_part.reshape(expert_ranks, rows_out, grad_width), small[:, None, :]], axis=1
    )
    sums = lax.all_to_all(wide_part, "experts", split_axis=0, concat_axis=0, tiled=True)
    sums = jnp.sum(sums.astype(f32), axis=0).astype(bf16)
    full = lax.all_gather(sums, "context", axis=0, tiled=False).astype(f32)
    qkv_grad = full[:, :rows_out, : 3 * share].reshape(ranks, rows_out, 3, share)
    qkv_grad = qkv_grad.transpose(1, 2, 0, 3).reshape(rows_out, 3, ranks * share)
    qkv_grad = qkv_grad[:, :, :width].reshape(rows_out, 3 * width)
    proj_grad = full[:, :rows_out, 3 * share :].transpose(1, 0, 2).reshape(rows_out, width)
    last = full[:, rows_out]
    first_grad = jnp.sum(last[:, :rows_out], axis=0)
    second_grad = jnp.sum(last[:, rows_out : 2 * rows_out], axis=0)
    table_grad = last[:, 2 * rows_out : 2 * rows_out + table_out * group]
    table_grad = table_grad.reshape(ranks, table_out, group).transpose(1, 0, 2)
    table_grad = table_grad.reshape(table_out, ranks * group)[:, :heads]
    return (
        block_output,
        input_grad,
        qkv_grad,
        proj_grad,
        first_grad,
        second_grad,
        table_grad,
        inner_grad,
        down_grad,
    )


def solution(mesh):
    placed = (
        P("experts", "context", None),
        P(),
        P(),
        P(),
        P(),
        P(),
        P("context", None),
        P("experts", "context"),
        P("experts", "context"),
        P("experts", "context"),
        P("experts", None, "context"),
        P("experts", "context", None),
        P("experts", "context", None),
    )
    return jax.shard_map(
        body,
        mesh=mesh,
        in_specs=placed,
        out_specs=(
            P("experts", "context", None),
            P("experts", "context", None),
            P("experts", None),
            P("experts", None),
            P("experts"),
            P("experts"),
            P("experts", None),
            P("experts", None, "context"),
            P("experts", "context", None),
        ),
        check_vma=False,
    )
```

```python
import functools
import math

import jax
import jax.numpy as jnp
from jax import lax
from jax.experimental import pallas as pl
from jax.experimental.pallas import tpu as pltpu
from jax.sharding import PartitionSpec as P

norm_eps = 1e-06
f32 = jnp.float32
bf16 = jnp.bfloat16
NT = (((1,), (1,)), ((), ()))
TN = (((0,), (0,)), ((), ()))
VMEM_BYTES = 48 * 1024 * 1024


def rms_scale(values, gain):
    factor = lax.rsqrt(jnp.mean(values * values, axis=-1, keepdims=True) + norm_eps)
    return values * factor * gain


def dot(a, b, dims=(((1,), (0,)), ((), ()))):
    return lax.dot_general(a, b, dims, preferred_element_type=f32)


def lane_lookup(row, index):
    source = jnp.broadcast_to(row, index.shape)
    numbers = lax.GatherDimensionNumbers(
        offset_dims=(),
        collapsed_slice_dims=(1,),
        start_index_map=(1,),
        operand_batching_dims=(0,),
        start_indices_batching_dims=(0,),
    )
    return lax.gather(
        source,
        index[..., None],
        numbers,
        slice_sizes=(1, 1),
        mode=lax.GatherScatterMode.PROMISE_IN_BOUNDS,
    )


def forward_kernel(scale, step, q_ref, k_ref, v_ref, table_ref, ids_ref, att_ref, prob_ref):
    total = ids_ref.shape[0]
    keys = k_ref[0]
    values = v_ref[0]
    row = table_ref[0]

    @pl.loop(0, total // step)
    def _(index):
        rows = pl.ds(pl.multiple_of(index * step, step), step)
        scores = dot(q_ref[0, rows, :], keys, NT) * scale
        ids = ids_ref[rows, :].astype(f32).astype(jnp.int32)
        bias = [lane_lookup(row, ids[:, at : at + 128]) for at in range(0, total, 128)]
        scores = scores + jnp.concatenate(bias, axis=1)
        expons = jnp.exp(scores - jnp.max(scores, axis=1, keepdims=True))
        probs = (expons / jnp.sum(expons, axis=1, keepdims=True)).astype(bf16)
        prob_ref[0, rows, :] = probs
        att_ref[0, rows, :] = dot(probs, values).astype(bf16)


def backward_kernel(
    scale, step, q_ref, k_ref, v_ref, att_ref, grad_ref, prob_ref, dq_ref, dk_ref, dv_ref, ds_ref,
    dk_sum, dv_sum,
):
    total = q_ref.shape[1]
    keys = k_ref[0]
    values = v_ref[0]
    dk_sum[...] = jnp.zeros_like(dk_sum)
    dv_sum[...] = jnp.zeros_like(dv_sum)

    @pl.loop(0, total // step)
    def _(index):
        rows = pl.ds(pl.multiple_of(index * step, step), step)
        grad = grad_ref[0, rows, :]
        probs = prob_ref[0, rows, :]
        delta = jnp.sum(
            grad.astype(f32) * att_ref[0, rows, :].astype(f32), axis=1, keepdims=True
        )
        d_scores = (probs.astype(f32) * (dot(grad, values, NT) - delta)).astype(bf16)
        ds_ref[0, rows, :] = d_scores
        dq_ref[0, rows, :] = (dot(d_scores, keys) * scale).astype(bf16)
        dk_sum[...] += dot(d_scores, q_ref[0, rows, :], TN)
        dv_sum[...] += dot(probs, grad, TN)

    dk_ref[0] = (dk_sum[...] * scale).astype(bf16)
    dv_ref[0] = dv_sum[...].astype(bf16)


def table_kernel(buckets, ds_ref, ids_ref, out_ref):
    total = ids_ref.shape[0]
    width = ids_ref.shape[1]
    group = 64

    def one_bucket(bucket, _):
        wanted = bucket.astype(f32).astype(bf16)

        def one_group(index, acc):
            rows = pl.ds(pl.multiple_of(index * group, group), group)
            picked = jnp.where(ids_ref[rows, :] == wanted, ds_ref[0, rows, :], jnp.zeros((), bf16))
            part = picked[0:16] + picked[16:32]
            for at in range(32, group, 16):
                part = part + picked[at : at + 16]
            return acc + part.astype(f32)

        acc = lax.fori_loop(0, total // group, one_group, jnp.zeros((16, width), f32), unroll=True)
        out_ref[0, pl.ds(bucket, 1), :] = jnp.sum(acc, axis=0, keepdims=True)
        return 0

    lax.fori_loop(0, buckets, one_bucket, 0)


def head_spec(rows, columns):
    return pl.BlockSpec((1, rows, columns), lambda h: (h, 0, 0))


def attend(q, k, v, table, ids):
    heads, total, size = q.shape
    scale = 1.0 / math.sqrt(size)
    return pl.pallas_call(
        functools.partial(forward_kernel, scale, 128),
        grid=(heads,),
        in_specs=[head_spec(total, size)] * 3
        + [head_spec(1, 128), pl.BlockSpec((total, total), lambda h: (0, 0))],
        out_specs=[head_spec(total, size), head_spec(total, total)],
        out_shape=[
            jax.ShapeDtypeStruct((heads, total, size), bf16),
            jax.ShapeDtypeStruct((heads, total, total), bf16),
        ],
        cost_estimate=pl.CostEstimate(
            flops=4 * heads * total * total * size,
            bytes_accessed=4 * heads * total * total,
            transcendentals=heads * total * total,
        ),
        compiler_params=pltpu.CompilerParams(vmem_limit_bytes=VMEM_BYTES),
        name="attend",
    )(q, k, v, table, ids)


def attend_back(q, k, v, att, grad, probs):
    heads, total, size = q.shape
    scale = 1.0 / math.sqrt(size)
    small = jax.ShapeDtypeStruct((heads, total, size), bf16)
    return pl.pallas_call(
        functools.partial(backward_kernel, scale, 128),
        grid=(heads,),
        in_specs=[head_spec(total, size)] * 5 + [head_spec(total, total)],
        out_specs=[head_spec(total, size)] * 3 + [head_spec(total, total)],
        out_shape=[small] * 3 + [jax.ShapeDtypeStruct((heads, total, total), bf16)],
        scratch_shapes=[pltpu.VMEM((total, size), f32)] * 2,
        cost_estimate=pl.CostEstimate(
            flops=8 * heads * total * total * size,
            bytes_accessed=8 * heads * total * total,
            transcendentals=0,
        ),
        compiler_params=pltpu.CompilerParams(vmem_limit_bytes=VMEM_BYTES),
        name="attend_back",
    )(q, k, v, att, grad, probs)


def table_sums(d_scores, ids, buckets):
    heads, total, _ = d_scores.shape
    sums = pl.pallas_call(
        functools.partial(table_kernel, buckets),
        grid=(heads,),
        in_specs=[head_spec(total, total), pl.BlockSpec((total, total), lambda h: (0, 0))],
        out_specs=head_spec(buckets, total),
        out_shape=jax.ShapeDtypeStruct((heads, buckets, total), f32),
        cost_estimate=pl.CostEstimate(
            flops=12000 * heads * total * total,
            bytes_accessed=4 * heads * total * total,
            transcendentals=0,
        ),
        compiler_params=pltpu.CompilerParams(vmem_limit_bytes=VMEM_BYTES),
        name="table_sums",
    )(d_scores, ids)
    return jnp.sum(sums, axis=2)


def body(
    block_input,
    first_gain,
    second_gain,
    qkv_weight,
    out_weight,
    rel_table,
    bucket_ids,
    expert_route,
    expert_slot,
    gate_value,
    expert_in,
    expert_down,
    upstream,
):
    ranks = lax.axis_size("context")
    me = lax.axis_index("context")
    expert_ranks = lax.axis_size("experts")
    local_rows, width = block_input.shape[1:]
    buckets, heads = rel_table.shape
    size = width // heads
    total = bucket_ids.shape[1]
    group = -(-heads // ranks)
    spare = group * ranks - heads
    share = group * size
    columns = width // ranks
    experts_local = expert_in.shape[0]
    experts_total = experts_local * expert_ranks
    capacity = max(4, 4 * local_rows // (3 * experts_total))
    slots = experts_total * capacity
    local_slots = experts_local * capacity

    features = block_input[0].astype(f32)
    gates = gate_value[0][:, None]
    grad_top = upstream[0].astype(f32)
    place = expert_route[0] * capacity + expert_slot[0]
    chosen = (place[None, :] == jnp.arange(slots, dtype=jnp.int32)[:, None]).astype(bf16)

    def send_rows(rows):
        spread = dot(chosen, rows).astype(bf16).reshape(expert_ranks, local_slots, -1)
        return lax.all_to_all(spread, "experts", split_axis=0, concat_axis=0, tiled=True)

    def share_rows(rows):
        return lax.all_gather(rows, "context", axis=0, tiled=True)

    shared = lax.all_gather(
        jnp.concatenate([block_input[0], bucket_ids.astype(bf16)], axis=1),
        "context",
        axis=0,
        tiled=True,
    )
    arrived_grads = send_rows((gates * grad_top).astype(bf16))
    shared, arrived_grads = lax.optimization_barrier((shared, arrived_grads))
    grad_rows = share_rows(arrived_grads)
    all_features = shared[:, :width].astype(f32)
    ids = shared[:, width:]
    normed = rms_scale(all_features, first_gain).astype(bf16)
    weight = jnp.pad(
        qkv_weight.reshape(width, 3, heads * size), ((0, 0), (0, 0), (0, spare * size))
    )
    my_weight = lax.dynamic_slice_in_dim(weight, me * share, share, 2).reshape(width, 3 * share)
    qkv = (
        dot(normed, my_weight)
        .astype(bf16)
        .reshape(total, 3, group, size)
        .transpose(1, 2, 0, 3)
    )
    q, k, v = qkv[0], qkv[1], qkv[2]
    table = jnp.pad(rel_table.T, ((0, spare), (0, 128 - buckets)))
    my_table = lax.dynamic_slice_in_dim(table, me * group, group, 0)[:, None, :]
    att, probs = attend(q, k, v, my_table, ids)
    all_att = lax.all_gather(
        att.transpose(1, 0, 2).reshape(total, share), "context", axis=0, tiled=False
    )
    all_att = all_att.transpose(1, 0, 2).reshape(total, ranks * share)[:, :width]
    attended = lax.dynamic_slice_in_dim(all_att, me * local_rows, local_rows, 0)
    middle = features + dot(attended, out_weight)
    second_normed = rms_scale(middle, second_gain)

    high_wide = lax.reduce_precision(second_normed, 8, 7)
    high = high_wide.astype(bf16)
    low = (second_normed - high_wide).astype(bf16)
    gathered = share_rows(send_rows(jnp.concatenate([high, low], axis=1)))

    blocks = ranks * expert_ranks
    many = blocks * local_slots
    number = jnp.arange(many, dtype=jnp.int32)
    source = number % (blocks * capacity)
    source = (source // capacity) * local_slots + (
        number // (blocks * capacity) * capacity + source % capacity
    )
    order = (source[:, None] == number[None, :]).astype(bf16)

    def by_expert(rows):
        moved = dot(order, rows.reshape(many, -1)).astype(bf16)
        return moved.reshape(experts_local, blocks * capacity, -1)

    def by_block(rows):
        moved = dot(order, rows.reshape(many, -1), TN).astype(bf16)
        return moved.reshape(ranks // 2, 2, expert_ranks, local_slots, -1)

    wide = by_expert(gathered)
    grads = by_expert(grad_rows)
    high_rows, low_rows = wide[:, :, :width], wide[:, :, width:]
    batched = functools.partial(jnp.einsum, preferred_element_type=f32)
    pre_act = batched("xnd,xdf->xnf", high_rows, expert_in) + batched(
        "xnd,xdf->xnf", low_rows, expert_in
    )
    hidden = jnp.maximum(pre_act, 0.0).astype(bf16)
    hidden_grad = batched("xnd,xfd->xnf", grads, expert_down)
    pre_grad = jnp.where(pre_act > 0.0, hidden_grad, 0.0).astype(bf16)
    forward_out = batched("xnf,xfd->xnd", hidden, expert_down).astype(bf16)
    back_in = batched("xnf,xdf->xnd", pre_grad, expert_in).astype(bf16)
    partial = by_block(jnp.concatenate([forward_out, back_in], axis=2))
    pair, chip, chips = me % 2, me // 2, ranks // 2
    held = lax.dynamic_index_in_dim(partial, pair, 1, keepdims=False)
    passed = lax.dynamic_index_in_dim(partial, 1 - pair, 1, keepdims=False)
    met = lax.ppermute(passed, "context", [(r, r ^ 1) for r in range(ranks)])
    both = held.astype(f32) + met.astype(f32)
    summed = lax.dynamic_index_in_dim(both, chip, 0, keepdims=False)
    for hop in range(1, chips):
        leaving = lax.dynamic_index_in_dim(both, (chip + hop) % chips, 0, keepdims=False)
        route = [(r, (r // 2 + hop) % chips * 2 + r % 2) for r in range(ranks)]
        summed = summed + lax.ppermute(leaving.astype(bf16), "context", route).astype(f32)
    summed = summed.astype(bf16)
    returned = lax.all_to_all(summed, "experts", split_axis=0, concat_axis=0, tiled=True)
    picked = dot(chosen, returned.reshape(slots, 2 * width), TN)
    inner_grad = batched("xnd,xnf->xdf", high_rows, pre_grad)
    down_grad = batched("xnf,xnd->xfd", hidden, grads)
    block_output = (middle + gates * picked[:, :width]).astype(bf16)[None]

    _, second_pull = jax.vjp(rms_scale, middle, second_gain)
    d_middle_norm, second_part = second_pull(picked[:, width:])
    d_middle = grad_top + d_middle_norm
    all_d_middle = lax.all_gather(d_middle.astype(bf16), "context", axis=0, tiled=True)

    out_rows = jnp.pad(out_weight, ((0, spare * size), (0, 0)))
    my_out = lax.dynamic_slice_in_dim(out_rows, me * share, share, 0)
    d_att = (
        dot(all_d_middle, my_out, NT).astype(bf16).reshape(total, group, size).transpose(1, 0, 2)
    )
    dq, dk, dv, d_scores = attend_back(q, k, v, att, d_att, probs)
    d_qkv = jnp.stack([dq, dk, dv]).transpose(2, 0, 1, 3).reshape(total, 3 * share)
    own = lax.all_to_all(
        d_qkv.reshape(ranks, local_rows, 3 * share),
        "context",
        split_axis=0,
        concat_axis=0,
        tiled=True,
    )
    own = own.reshape(ranks, local_rows, 3, share).transpose(1, 2, 0, 3)
    own = own.reshape(local_rows, 3, ranks * share)[:, :, :width].reshape(local_rows, 3 * width)
    d_first = dot(own, qkv_weight, NT)
    _, first_pull = jax.vjp(rms_scale, features, first_gain)
    d_input_norm, first_part = first_pull(d_first)
    input_grad = (d_middle + d_input_norm)[None]

    my_d_middle = lax.dynamic_slice_in_dim(all_d_middle, me * columns, columns, 1)
    qkv_part = dot(normed, d_qkv, TN)
    proj_part = dot(all_att, my_d_middle, TN)
    table_part = table_sums(d_scores, ids, buckets).T
    wide_part = jnp.concatenate([qkv_part, proj_part], axis=1).astype(bf16)
    grad_width = 3 * share + columns
    rows_out = width // expert_ranks
    table_out = buckets // expert_ranks
    small = jnp.concatenate(
        [
            first_part.reshape(expert_ranks, rows_out),
            second_part.reshape(expert_ranks, rows_out),
            table_part.reshape(expert_ranks, table_out * group),
        ],
        axis=1,
    ).astype(bf16)
    small = jnp.pad(small, ((0, 0), (0, grad_width - small.shape[1])))
    wide_part = jnp.concatenate(
        [wide_part.reshape(expert_ranks, rows_out, grad_width), small[:, None, :]], axis=1
    )
    sums = lax.all_to_all(wide_part, "experts", split_axis=0, concat_axis=0, tiled=True)
    sums = jnp.sum(sums.astype(f32), axis=0).astype(bf16)
    full = lax.all_gather(sums, "context", axis=0, tiled=False).astype(f32)
    qkv_grad = full[:, :rows_out, : 3 * share].reshape(ranks, rows_out, 3, share)
    qkv_grad = qkv_grad.transpose(1, 2, 0, 3).reshape(rows_out, 3, ranks * share)
    qkv_grad = qkv_grad[:, :, :width].reshape(rows_out, 3 * width)
    proj_grad = full[:, :rows_out, 3 * share :].transpose(1, 0, 2).reshape(rows_out, width)
    last = full[:, rows_out]
    first_grad = jnp.sum(last[:, :rows_out], axis=0)
    second_grad = jnp.sum(last[:, rows_out : 2 * rows_out], axis=0)
    table_grad = last[:, 2 * rows_out : 2 * rows_out + table_out * group]
    table_grad = table_grad.reshape(ranks, table_out, group).transpose(1, 0, 2)
    table_grad = table_grad.reshape(table_out, ranks * group)[:, :heads]
    return (
        block_output,
        input_grad,
        qkv_grad,
        proj_grad,
        first_grad,
        second_grad,
        table_grad,
        inner_grad,
        down_grad,
    )


def solution(mesh):
    placed = (
        P("experts", "context", None),
        P(),
        P(),
        P(),
        P(),
        P(),
        P("context", None),
        P("experts", "context"),
        P("experts", "context"),
        P("experts", "context"),
        P("experts", None, "context"),
        P("experts", "context", None),
        P("experts", "context", None),
    )
    return jax.shard_map(
        body,
        mesh=mesh,
        in_specs=placed,
        out_specs=(
            P("experts", "context", None),
            P("experts", "context", None),
            P("experts", None),
            P("experts", None),
            P("experts"),
            P("experts"),
            P("experts", None),
            P("experts", None, "context"),
            P("experts", "context", None),
        ),
        check_vma=False,
    )
```

```python
import functools
import math

import jax
import jax.numpy as jnp
from jax import lax
from jax.experimental import pallas as pl
from jax.experimental.pallas import tpu as pltpu
from jax.sharding import PartitionSpec as P

norm_eps = 1e-06
f32 = jnp.float32
bf16 = jnp.bfloat16
NT = (((1,), (1,)), ((), ()))
TN = (((0,), (0,)), ((), ()))
VMEM_BYTES = 48 * 1024 * 1024


def rms_scale(values, gain):
    factor = lax.rsqrt(jnp.mean(values * values, axis=-1, keepdims=True) + norm_eps)
    return values * factor * gain


def dot(a, b, dims=(((1,), (0,)), ((), ()))):
    return lax.dot_general(a, b, dims, preferred_element_type=f32)


def lane_lookup(row, index):
    source = jnp.broadcast_to(row, index.shape)
    numbers = lax.GatherDimensionNumbers(
        offset_dims=(),
        collapsed_slice_dims=(1,),
        start_index_map=(1,),
        operand_batching_dims=(0,),
        start_indices_batching_dims=(0,),
    )
    return lax.gather(
        source,
        index[..., None],
        numbers,
        slice_sizes=(1, 1),
        mode=lax.GatherScatterMode.PROMISE_IN_BOUNDS,
    )


def forward_kernel(scale, step, q_ref, k_ref, v_ref, table_ref, ids_ref, att_ref, prob_ref):
    total = ids_ref.shape[0]
    keys = k_ref[0]
    values = v_ref[0]
    row = table_ref[0]

    @pl.loop(0, total // step)
    def _(index):
        rows = pl.ds(pl.multiple_of(index * step, step), step)
        scores = dot(q_ref[0, rows, :], keys, NT) * scale
        ids = ids_ref[rows, :].astype(f32).astype(jnp.int32)
        bias = [lane_lookup(row, ids[:, at : at + 128]) for at in range(0, total, 128)]
        scores = scores + jnp.concatenate(bias, axis=1)
        expons = jnp.exp(scores - jnp.max(scores, axis=1, keepdims=True))
        probs = (expons / jnp.sum(expons, axis=1, keepdims=True)).astype(bf16)
        prob_ref[0, rows, :] = probs
        att_ref[0, rows, :] = dot(probs, values).astype(bf16)


def backward_kernel(
    scale, step, q_ref, k_ref, v_ref, att_ref, grad_ref, prob_ref, dq_ref, dk_ref, dv_ref, ds_ref,
    dk_sum, dv_sum,
):
    total = q_ref.shape[1]
    keys = k_ref[0]
    values = v_ref[0]
    dk_sum[...] = jnp.zeros_like(dk_sum)
    dv_sum[...] = jnp.zeros_like(dv_sum)

    @pl.loop(0, total // step)
    def _(index):
        rows = pl.ds(pl.multiple_of(index * step, step), step)
        grad = grad_ref[0, rows, :]
        probs = prob_ref[0, rows, :]
        delta = jnp.sum(
            grad.astype(f32) * att_ref[0, rows, :].astype(f32), axis=1, keepdims=True
        )
        d_scores = (probs.astype(f32) * (dot(grad, values, NT) - delta)).astype(bf16)
        ds_ref[0, rows, :] = d_scores
        dq_ref[0, rows, :] = (dot(d_scores, keys) * scale).astype(bf16)
        dk_sum[...] += dot(d_scores, q_ref[0, rows, :], TN)
        dv_sum[...] += dot(probs, grad, TN)

    dk_ref[0] = (dk_sum[...] * scale).astype(bf16)
    dv_ref[0] = dv_sum[...].astype(bf16)


def table_kernel(buckets, ds_ref, ids_ref, out_ref):
    total = ids_ref.shape[0]
    width = ids_ref.shape[1]
    group = 64

    def one_bucket(bucket, _):
        wanted = bucket.astype(f32).astype(bf16)

        def one_group(index, acc):
            rows = pl.ds(pl.multiple_of(index * group, group), group)
            picked = jnp.where(ids_ref[rows, :] == wanted, ds_ref[0, rows, :], jnp.zeros((), bf16))
            part = picked[0:16] + picked[16:32]
            for at in range(32, group, 16):
                part = part + picked[at : at + 16]
            return acc + part.astype(f32)

        acc = lax.fori_loop(0, total // group, one_group, jnp.zeros((16, width), f32), unroll=True)
        out_ref[0, pl.ds(bucket, 1), :] = jnp.sum(acc, axis=0, keepdims=True)
        return 0

    lax.fori_loop(0, buckets, one_bucket, 0)


def head_spec(rows, columns):
    return pl.BlockSpec((1, rows, columns), lambda h: (h, 0, 0))


def attend(q, k, v, table, ids):
    heads, total, size = q.shape
    scale = 1.0 / math.sqrt(size)
    return pl.pallas_call(
        functools.partial(forward_kernel, scale, 128),
        grid=(heads,),
        in_specs=[head_spec(total, size)] * 3
        + [head_spec(1, 128), pl.BlockSpec((total, total), lambda h: (0, 0))],
        out_specs=[head_spec(total, size), head_spec(total, total)],
        out_shape=[
            jax.ShapeDtypeStruct((heads, total, size), bf16),
            jax.ShapeDtypeStruct((heads, total, total), bf16),
        ],
        cost_estimate=pl.CostEstimate(
            flops=4 * heads * total * total * size,
            bytes_accessed=4 * heads * total * total,
            transcendentals=heads * total * total,
        ),
        compiler_params=pltpu.CompilerParams(vmem_limit_bytes=VMEM_BYTES),
        name="attend",
    )(q, k, v, table, ids)


def attend_back(q, k, v, att, grad, probs):
    heads, total, size = q.shape
    scale = 1.0 / math.sqrt(size)
    small = jax.ShapeDtypeStruct((heads, total, size), bf16)
    return pl.pallas_call(
        functools.partial(backward_kernel, scale, 128),
        grid=(heads,),
        in_specs=[head_spec(total, size)] * 5 + [head_spec(total, total)],
        out_specs=[head_spec(total, size)] * 3 + [head_spec(total, total)],
        out_shape=[small] * 3 + [jax.ShapeDtypeStruct((heads, total, total), bf16)],
        scratch_shapes=[pltpu.VMEM((total, size), f32)] * 2,
        cost_estimate=pl.CostEstimate(
            flops=8 * heads * total * total * size,
            bytes_accessed=8 * heads * total * total,
            transcendentals=0,
        ),
        compiler_params=pltpu.CompilerParams(vmem_limit_bytes=VMEM_BYTES),
        name="attend_back",
    )(q, k, v, att, grad, probs)


def table_sums(d_scores, ids, buckets):
    heads, total, _ = d_scores.shape
    sums = pl.pallas_call(
        functools.partial(table_kernel, buckets),
        grid=(heads,),
        in_specs=[head_spec(total, total), pl.BlockSpec((total, total), lambda h: (0, 0))],
        out_specs=head_spec(buckets, total),
        out_shape=jax.ShapeDtypeStruct((heads, buckets, total), f32),
        cost_estimate=pl.CostEstimate(
            flops=12000 * heads * total * total,
            bytes_accessed=4 * heads * total * total,
            transcendentals=0,
        ),
        compiler_params=pltpu.CompilerParams(vmem_limit_bytes=VMEM_BYTES),
        name="table_sums",
    )(d_scores, ids)
    return jnp.sum(sums, axis=2)


def body(
    block_input,
    first_gain,
    second_gain,
    qkv_weight,
    out_weight,
    rel_table,
    bucket_ids,
    expert_route,
    expert_slot,
    gate_value,
    expert_in,
    expert_down,
    upstream,
):
    ranks = lax.axis_size("context")
    me = lax.axis_index("context")
    expert_ranks = lax.axis_size("experts")
    local_rows, width = block_input.shape[1:]
    buckets, heads = rel_table.shape
    size = width // heads
    total = bucket_ids.shape[1]
    group = -(-heads // ranks)
    spare = group * ranks - heads
    share = group * size
    columns = width // ranks
    experts_local = expert_in.shape[0]
    experts_total = experts_local * expert_ranks
    capacity = max(4, 4 * local_rows // (3 * experts_total))
    slots = experts_total * capacity
    local_slots = experts_local * capacity

    features = block_input[0].astype(f32)
    gates = gate_value[0][:, None]
    grad_top = upstream[0].astype(f32)
    place = (expert_route[0] % experts_local) * capacity + expert_slot[0]
    place = place * expert_ranks + expert_route[0] // experts_local
    chosen = (place[None, :] == jnp.arange(slots, dtype=jnp.int32)[:, None]).astype(bf16)

    def send_rows(rows):
        spread = dot(chosen, rows).astype(bf16).reshape(local_slots, expert_ranks, -1)
        moved = lax.all_to_all(spread, "experts", split_axis=1, concat_axis=1, tiled=True)
        return moved.reshape(slots, -1)

    def share_rows(rows):
        return lax.all_gather(rows, "context", axis=0, tiled=False)

    shared = lax.all_gather(
        jnp.concatenate([block_input[0], bucket_ids.astype(bf16)], axis=1),
        "context",
        axis=0,
        tiled=True,
    )
    arrived_grads = send_rows((gates * grad_top).astype(bf16))
    shared, arrived_grads = lax.optimization_barrier((shared, arrived_grads))
    grad_rows = share_rows(arrived_grads)
    all_features = shared[:, :width].astype(f32)
    ids = shared[:, width:]
    normed = rms_scale(all_features, first_gain).astype(bf16)
    weight = jnp.pad(
        qkv_weight.reshape(width, 3, heads * size), ((0, 0), (0, 0), (0, spare * size))
    )
    my_weight = lax.dynamic_slice_in_dim(weight, me * share, share, 2).reshape(width, 3 * share)
    qkv = (
        dot(normed, my_weight)
        .astype(bf16)
        .reshape(total, 3, group, size)
        .transpose(1, 2, 0, 3)
    )
    q, k, v = qkv[0], qkv[1], qkv[2]
    table = jnp.pad(rel_table.T, ((0, spare), (0, 128 - buckets)))
    my_table = lax.dynamic_slice_in_dim(table, me * group, group, 0)[:, None, :]
    att, probs = attend(q, k, v, my_table, ids)
    all_att = lax.all_gather(
        att.transpose(1, 0, 2).reshape(total, share), "context", axis=0, tiled=False
    )
    all_att = all_att.transpose(1, 0, 2).reshape(total, ranks * share)[:, :width]
    attended = lax.dynamic_slice_in_dim(all_att, me * local_rows, local_rows, 0)
    middle = features + dot(attended, out_weight)
    second_normed = rms_scale(middle, second_gain)

    high_wide = lax.reduce_precision(second_normed, 8, 7)
    high = high_wide.astype(bf16)
    low = (second_normed - high_wide).astype(bf16)
    gathered = share_rows(send_rows(jnp.concatenate([high, low], axis=1)))

    per_expert = capacity * expert_ranks

    def by_expert(rows):
        rows = rows.reshape(ranks, experts_local, per_expert, -1).transpose(1, 0, 2, 3)
        return rows.reshape(experts_local, ranks * per_expert, -1)

    def by_block(rows):
        rows = rows.reshape(experts_local, ranks, per_expert, -1).transpose(1, 0, 2, 3)
        return rows.reshape(ranks // 2, 2, slots, -1)

    wide = by_expert(gathered)
    grads = by_expert(grad_rows)
    high_rows, low_rows = wide[:, :, :width], wide[:, :, width:]
    batched = functools.partial(jnp.einsum, preferred_element_type=f32)
    pre_act = batched("xnd,xdf->xnf", high_rows, expert_in) + batched(
        "xnd,xdf->xnf", low_rows, expert_in
    )
    hidden = jnp.maximum(pre_act, 0.0).astype(bf16)
    hidden_grad = batched("xnd,xfd->xnf", grads, expert_down)
    pre_grad = jnp.where(pre_act > 0.0, hidden_grad, 0.0).astype(bf16)
    forward_out = batched("xnf,xfd->xnd", hidden, expert_down).astype(bf16)
    back_in = batched("xnf,xdf->xnd", pre_grad, expert_in).astype(bf16)
    partial = by_block(jnp.concatenate([forward_out, back_in], axis=2))
    pair, chip, chips = me % 2, me // 2, ranks // 2
    held = lax.dynamic_index_in_dim(partial, pair, 1, keepdims=False)
    passed = lax.dynamic_index_in_dim(partial, 1 - pair, 1, keepdims=False)
    met = lax.ppermute(passed, "context", [(r, r ^ 1) for r in range(ranks)])
    both = held.astype(f32) + met.astype(f32)
    summed = lax.dynamic_index_in_dim(both, chip, 0, keepdims=False)
    for hop in range(1, chips):
        leaving = lax.dynamic_index_in_dim(both, (chip + hop) % chips, 0, keepdims=False)
        route = [(r, (r // 2 + hop) % chips * 2 + r % 2) for r in range(ranks)]
        summed = summed + lax.ppermute(leaving.astype(bf16), "context", route).astype(f32)
    summed = summed.astype(bf16)
    returned = lax.all_to_all(
        summed.reshape(local_slots, expert_ranks, 2 * width),
        "experts",
        split_axis=1,
        concat_axis=1,
        tiled=True,
    )
    picked = dot(chosen, returned.reshape(slots, 2 * width), TN)
    inner_grad = batched("xnd,xnf->xdf", high_rows, pre_grad)
    down_grad = batched("xnf,xnd->xfd", hidden, grads)
    block_output = (middle + gates * picked[:, :width]).astype(bf16)[None]

    _, second_pull = jax.vjp(rms_scale, middle, second_gain)
    d_middle_norm, second_part = second_pull(picked[:, width:])
    d_middle = grad_top + d_middle_norm
    all_d_middle = lax.all_gather(d_middle.astype(bf16), "context", axis=0, tiled=True)

    out_rows = jnp.pad(out_weight, ((0, spare * size), (0, 0)))
    my_out = lax.dynamic_slice_in_dim(out_rows, me * share, share, 0)
    d_att = (
        dot(all_d_middle, my_out, NT).astype(bf16).reshape(total, group, size).transpose(1, 0, 2)
    )
    dq, dk, dv, d_scores = attend_back(q, k, v, att, d_att, probs)
    d_qkv = jnp.stack([dq, dk, dv]).transpose(2, 0, 1, 3).reshape(total, 3 * share)
    my_d_middle = lax.dynamic_slice_in_dim(all_d_middle, me * columns, columns, 1)
    qkv_part = dot(normed, d_qkv, TN)
    proj_part = dot(all_att, my_d_middle, TN)
    d_scores, qkv_part = lax.optimization_barrier((d_scores, qkv_part))
    table_part = table_sums(d_scores, ids, buckets).T
    wide_part = jnp.concatenate([qkv_part, proj_part], axis=1).astype(bf16)
    grad_width = 3 * share + columns
    rows_out = width // expert_ranks
    table_out = buckets // expert_ranks
    small = jnp.concatenate(
        [
            second_part.reshape(expert_ranks, rows_out),
            table_part.reshape(expert_ranks, table_out * group),
        ],
        axis=1,
    ).astype(bf16)
    small = jnp.pad(small, ((0, 0), (0, grad_width - small.shape[1])))
    wide_part = jnp.concatenate(
        [wide_part.reshape(expert_ranks, rows_out, grad_width), small[:, None, :]], axis=1
    )
    sums = lax.all_to_all(wide_part, "experts", split_axis=0, concat_axis=0, tiled=True)
    outgoing = d_qkv.reshape(ranks, local_rows, 3 * share)
    own = lax.dynamic_update_index_in_dim(
        jnp.zeros_like(outgoing), lax.dynamic_index_in_dim(outgoing, me, 0), me, 0
    )
    for hop in range(1, ranks):
        leaving = lax.dynamic_index_in_dim(outgoing, (me + hop) % ranks, 0)
        met = lax.ppermute(leaving, "context", [(r, (r + hop) % ranks) for r in range(ranks)])
        own = lax.dynamic_update_index_in_dim(own, met, (me - hop) % ranks, 0)
    own = own.reshape(ranks, local_rows, 3, share).transpose(1, 2, 0, 3)
    own = own.reshape(local_rows, 3, ranks * share)[:, :, :width].reshape(local_rows, 3 * width)
    d_first = dot(own, qkv_weight, NT)
    _, first_pull = jax.vjp(rms_scale, features, first_gain)
    d_input_norm, first_part = first_pull(d_first)
    input_grad = (d_middle + d_input_norm)[None]

    first_rows = lax.all_to_all(
        first_part.astype(bf16).reshape(expert_ranks, 1, rows_out),
        "experts",
        split_axis=0,
        concat_axis=0,
        tiled=True,
    )
    first_sum = jnp.sum(first_rows.astype(f32), axis=0)
    first_row = jnp.pad(first_sum, ((0, 0), (0, grad_width - rows_out)))
    sums = jnp.concatenate([jnp.sum(sums.astype(f32), axis=0), first_row], axis=0).astype(bf16)
    full = lax.all_gather(sums, "context", axis=0, tiled=False).astype(f32)
    qkv_grad = full[:, :rows_out, : 3 * share].reshape(ranks, rows_out, 3, share)
    qkv_grad = qkv_grad.transpose(1, 2, 0, 3).reshape(rows_out, 3, ranks * share)
    qkv_grad = qkv_grad[:, :, :width].reshape(rows_out, 3 * width)
    proj_grad = full[:, :rows_out, 3 * share :].transpose(1, 0, 2).reshape(rows_out, width)
    last = full[:, rows_out]
    first_grad = jnp.sum(full[:, rows_out + 1, :rows_out], axis=0)
    second_grad = jnp.sum(last[:, :rows_out], axis=0)
    table_grad = last[:, rows_out : rows_out + table_out * group]
    table_grad = table_grad.reshape(ranks, table_out, group).transpose(1, 0, 2)
    table_grad = table_grad.reshape(table_out, ranks * group)[:, :heads]
    return (
        block_output,
        input_grad,
        qkv_grad,
        proj_grad,
        first_grad,
        second_grad,
        table_grad,
        inner_grad,
        down_grad,
    )


def solution(mesh):
    placed = (
        P("experts", "context", None),
        P(),
        P(),
        P(),
        P(),
        P(),
        P("context", None),
        P("experts", "context"),
        P("experts", "context"),
        P("experts", "context"),
        P("experts", None, "context"),
        P("experts", "context", None),
        P("experts", "context", None),
    )
    return jax.shard_map(
        body,
        mesh=mesh,
        in_specs=placed,
        out_specs=(
            P("experts", "context", None),
            P("experts", "context", None),
            P("experts", None),
            P("experts", None),
            P("experts"),
            P("experts"),
            P("experts", None),
            P("experts", None, "context"),
            P("experts", "context", None),
        ),
        check_vma=False,
    )
```

```python
import functools
import math

import jax
import jax.numpy as jnp
from jax import lax
from jax.experimental import pallas as pl
from jax.experimental.pallas import tpu as pltpu
from jax.sharding import PartitionSpec as P

norm_eps = 1e-06
f32 = jnp.float32
bf16 = jnp.bfloat16
NT = (((1,), (1,)), ((), ()))
TN = (((0,), (0,)), ((), ()))
VMEM_BYTES = 48 * 1024 * 1024


def rms_scale(values, gain):
    factor = lax.rsqrt(jnp.mean(values * values, axis=-1, keepdims=True) + norm_eps)
    return values * factor * gain


def dot(a, b, dims=(((1,), (0,)), ((), ()))):
    return lax.dot_general(a, b, dims, preferred_element_type=f32)


def lane_lookup(row, index):
    source = jnp.broadcast_to(row, index.shape)
    numbers = lax.GatherDimensionNumbers(
        offset_dims=(),
        collapsed_slice_dims=(1,),
        start_index_map=(1,),
        operand_batching_dims=(0,),
        start_indices_batching_dims=(0,),
    )
    return lax.gather(
        source,
        index[..., None],
        numbers,
        slice_sizes=(1, 1),
        mode=lax.GatherScatterMode.PROMISE_IN_BOUNDS,
    )


def forward_kernel(scale, step, q_ref, k_ref, v_ref, table_ref, ids_ref, att_ref, prob_ref):
    total = ids_ref.shape[0]
    keys = k_ref[0]
    values = v_ref[0]
    row = table_ref[0]

    @pl.loop(0, total // step)
    def _(index):
        rows = pl.ds(pl.multiple_of(index * step, step), step)
        scores = dot(q_ref[0, rows, :], keys, NT) * scale
        ids = ids_ref[rows, :].astype(f32).astype(jnp.int32)
        bias = [lane_lookup(row, ids[:, at : at + 128]) for at in range(0, total, 128)]
        scores = scores + jnp.concatenate(bias, axis=1)
        expons = jnp.exp(scores - jnp.max(scores, axis=1, keepdims=True))
        probs = (expons / jnp.sum(expons, axis=1, keepdims=True)).astype(bf16)
        prob_ref[0, rows, :] = probs
        att_ref[0, rows, :] = dot(probs, values).astype(bf16)


def backward_kernel(
    scale, step, q_ref, k_ref, v_ref, att_ref, grad_ref, prob_ref, dq_ref, dk_ref, dv_ref, ds_ref,
    dk_sum, dv_sum,
):
    total = q_ref.shape[1]
    keys = k_ref[0]
    values = v_ref[0]
    dk_sum[...] = jnp.zeros_like(dk_sum)
    dv_sum[...] = jnp.zeros_like(dv_sum)

    @pl.loop(0, total // step)
    def _(index):
        rows = pl.ds(pl.multiple_of(index * step, step), step)
        grad = grad_ref[0, rows, :]
        probs = prob_ref[0, rows, :]
        delta = jnp.sum(
            grad.astype(f32) * att_ref[0, rows, :].astype(f32), axis=1, keepdims=True
        )
        d_scores = (probs.astype(f32) * (dot(grad, values, NT) - delta)).astype(bf16)
        ds_ref[0, rows, :] = d_scores
        dq_ref[0, rows, :] = (dot(d_scores, keys) * scale).astype(bf16)
        dk_sum[...] += dot(d_scores, q_ref[0, rows, :], TN)
        dv_sum[...] += dot(probs, grad, TN)

    dk_ref[0] = (dk_sum[...] * scale).astype(bf16)
    dv_ref[0] = dv_sum[...].astype(bf16)


def table_kernel(buckets, ds_ref, ids_ref, out_ref):
    total = ids_ref.shape[0]
    width = ids_ref.shape[1]
    group = 64

    def one_bucket(bucket, _):
        wanted = bucket.astype(f32).astype(bf16)

        def one_group(index, acc):
            rows = pl.ds(pl.multiple_of(index * group, group), group)
            picked = jnp.where(ids_ref[rows, :] == wanted, ds_ref[0, rows, :], jnp.zeros((), bf16))
            part = picked[0:16] + picked[16:32]
            for at in range(32, group, 16):
                part = part + picked[at : at + 16]
            return acc + part.astype(f32)

        acc = lax.fori_loop(0, total // group, one_group, jnp.zeros((16, width), f32), unroll=True)
        out_ref[0, pl.ds(bucket, 1), :] = jnp.sum(acc, axis=0, keepdims=True)
        return 0

    lax.fori_loop(0, buckets, one_bucket, 0)


def head_spec(rows, columns):
    return pl.BlockSpec((1, rows, columns), lambda h: (h, 0, 0))


def attend(q, k, v, table, ids):
    heads, total, size = q.shape
    scale = 1.0 / math.sqrt(size)
    return pl.pallas_call(
        functools.partial(forward_kernel, scale, 128),
        grid=(heads,),
        in_specs=[head_spec(total, size)] * 3
        + [head_spec(1, 128), pl.BlockSpec((total, total), lambda h: (0, 0))],
        out_specs=[head_spec(total, size), head_spec(total, total)],
        out_shape=[
            jax.ShapeDtypeStruct((heads, total, size), bf16),
            jax.ShapeDtypeStruct((heads, total, total), bf16),
        ],
        cost_estimate=pl.CostEstimate(
            flops=4 * heads * total * total * size,
            bytes_accessed=4 * heads * total * total,
            transcendentals=heads * total * total,
        ),
        compiler_params=pltpu.CompilerParams(vmem_limit_bytes=VMEM_BYTES),
        name="attend",
    )(q, k, v, table, ids)


def attend_back(q, k, v, att, grad, probs):
    heads, total, size = q.shape
    scale = 1.0 / math.sqrt(size)
    small = jax.ShapeDtypeStruct((heads, total, size), bf16)
    return pl.pallas_call(
        functools.partial(backward_kernel, scale, 128),
        grid=(heads,),
        in_specs=[head_spec(total, size)] * 5 + [head_spec(total, total)],
        out_specs=[head_spec(total, size)] * 3 + [head_spec(total, total)],
        out_shape=[small] * 3 + [jax.ShapeDtypeStruct((heads, total, total), bf16)],
        scratch_shapes=[pltpu.VMEM((total, size), f32)] * 2,
        cost_estimate=pl.CostEstimate(
            flops=8 * heads * total * total * size,
            bytes_accessed=8 * heads * total * total,
            transcendentals=0,
        ),
        compiler_params=pltpu.CompilerParams(vmem_limit_bytes=VMEM_BYTES),
        name="attend_back",
    )(q, k, v, att, grad, probs)


def table_sums(d_scores, ids, buckets):
    heads, total, _ = d_scores.shape
    sums = pl.pallas_call(
        functools.partial(table_kernel, buckets),
        grid=(heads,),
        in_specs=[head_spec(total, total), pl.BlockSpec((total, total), lambda h: (0, 0))],
        out_specs=head_spec(buckets, total),
        out_shape=jax.ShapeDtypeStruct((heads, buckets, total), f32),
        cost_estimate=pl.CostEstimate(
            flops=12000 * heads * total * total,
            bytes_accessed=4 * heads * total * total,
            transcendentals=0,
        ),
        compiler_params=pltpu.CompilerParams(vmem_limit_bytes=VMEM_BYTES),
        name="table_sums",
    )(d_scores, ids)
    return jnp.sum(sums, axis=2)


def body(
    block_input,
    first_gain,
    second_gain,
    qkv_weight,
    out_weight,
    rel_table,
    bucket_ids,
    expert_route,
    expert_slot,
    gate_value,
    expert_in,
    expert_down,
    upstream,
):
    ranks = lax.axis_size("context")
    me = lax.axis_index("context")
    expert_ranks = lax.axis_size("experts")
    local_rows, width = block_input.shape[1:]
    buckets, heads = rel_table.shape
    size = width // heads
    total = bucket_ids.shape[1]
    group = -(-heads // ranks)
    spare = group * ranks - heads
    share = group * size
    columns = width // ranks
    experts_local = expert_in.shape[0]
    experts_total = experts_local * expert_ranks
    capacity = max(4, 4 * local_rows // (3 * experts_total))
    slots = experts_total * capacity
    local_slots = experts_local * capacity

    features = block_input[0].astype(f32)
    gates = gate_value[0][:, None]
    grad_top = upstream[0].astype(f32)
    place = (expert_route[0] % experts_local) * capacity + expert_slot[0]
    place = place * expert_ranks + expert_route[0] // experts_local
    chosen = (place[None, :] == jnp.arange(slots, dtype=jnp.int32)[:, None]).astype(bf16)

    def send_rows(rows):
        spread = dot(chosen, rows).astype(bf16).reshape(local_slots, expert_ranks, -1)
        moved = lax.all_to_all(spread, "experts", split_axis=1, concat_axis=1, tiled=True)
        return moved.reshape(slots, -1)

    def share_rows(rows):
        return lax.all_gather(rows, "context", axis=0, tiled=False)

    shared = lax.all_gather(
        jnp.concatenate([block_input[0], bucket_ids.astype(bf16)], axis=1),
        "context",
        axis=0,
        tiled=True,
    )
    arrived_grads = send_rows((gates * grad_top).astype(bf16))
    shared, arrived_grads = lax.optimization_barrier((shared, arrived_grads))
    grad_rows = share_rows(arrived_grads)
    all_features = shared[:, :width].astype(f32)
    ids = shared[:, width:]
    normed = rms_scale(all_features, first_gain).astype(bf16)
    weight = jnp.pad(
        qkv_weight.reshape(width, 3, heads * size), ((0, 0), (0, 0), (0, spare * size))
    )
    my_weight = lax.dynamic_slice_in_dim(weight, me * share, share, 2).reshape(width, 3 * share)
    qkv = (
        dot(normed, my_weight)
        .astype(bf16)
        .reshape(total, 3, group, size)
        .transpose(1, 2, 0, 3)
    )
    q, k, v = qkv[0], qkv[1], qkv[2]
    table = jnp.pad(rel_table.T, ((0, spare), (0, 128 - buckets)))
    my_table = lax.dynamic_slice_in_dim(table, me * group, group, 0)[:, None, :]
    att, probs = attend(q, k, v, my_table, ids)
    all_att = lax.all_gather(
        att.transpose(1, 0, 2).reshape(total, share), "context", axis=0, tiled=False
    )
    all_att = all_att.transpose(1, 0, 2).reshape(total, ranks * share)[:, :width]
    attended = lax.dynamic_slice_in_dim(all_att, me * local_rows, local_rows, 0)
    middle = features + dot(attended, out_weight)
    second_normed = rms_scale(middle, second_gain)

    high_wide = lax.reduce_precision(second_normed, 8, 7)
    high = high_wide.astype(bf16)
    low = (second_normed - high_wide).astype(bf16)
    gathered = share_rows(send_rows(jnp.concatenate([high, low], axis=1)))

    per_expert = capacity * expert_ranks

    def by_expert(rows):
        rows = rows.reshape(ranks, experts_local, per_expert, -1).transpose(1, 0, 2, 3)
        return rows.reshape(experts_local, ranks * per_expert, -1)

    def by_block(rows):
        rows = rows.reshape(experts_local, ranks, per_expert, -1).transpose(1, 0, 2, 3)
        return rows.reshape(ranks // 2, 2, slots, -1)

    wide = by_expert(gathered)
    grads = by_expert(grad_rows)
    high_rows, low_rows = wide[:, :, :width], wide[:, :, width:]
    batched = functools.partial(jnp.einsum, preferred_element_type=f32)
    pre_act = batched("xnd,xdf->xnf", high_rows, expert_in) + batched(
        "xnd,xdf->xnf", low_rows, expert_in
    )
    hidden = jnp.maximum(pre_act, 0.0).astype(bf16)
    hidden_grad = batched("xnd,xfd->xnf", grads, expert_down)
    pre_grad = jnp.where(pre_act > 0.0, hidden_grad, 0.0).astype(bf16)
    forward_out = batched("xnf,xfd->xnd", hidden, expert_down).astype(bf16)
    back_in = batched("xnf,xdf->xnd", pre_grad, expert_in).astype(bf16)
    partial = by_block(jnp.concatenate([forward_out, back_in], axis=2))
    pair, chip, chips = me % 2, me // 2, ranks // 2
    held = lax.dynamic_index_in_dim(partial, pair, 1, keepdims=False)
    passed = lax.dynamic_index_in_dim(partial, 1 - pair, 1, keepdims=False)
    met = lax.ppermute(passed, "context", [(r, r ^ 1) for r in range(ranks)])
    both = held.astype(f32) + met.astype(f32)
    summed = lax.dynamic_index_in_dim(both, chip, 0, keepdims=False)
    for hop in range(1, chips):
        leaving = lax.dynamic_index_in_dim(both, (chip + hop) % chips, 0, keepdims=False)
        route = [(r, (r // 2 + hop) % chips * 2 + r % 2) for r in range(ranks)]
        summed = summed + lax.ppermute(leaving.astype(bf16), "context", route).astype(f32)
    summed = summed.astype(bf16)
    returned = lax.all_to_all(
        summed.reshape(local_slots, expert_ranks, 2 * width),
        "experts",
        split_axis=1,
        concat_axis=1,
        tiled=True,
    )
    picked = dot(chosen, returned.reshape(slots, 2 * width), TN)
    inner_grad = batched("xnd,xnf->xdf", high_rows, pre_grad)
    down_grad = batched("xnf,xnd->xfd", hidden, grads)
    block_output = (middle + gates * picked[:, :width]).astype(bf16)[None]

    _, second_pull = jax.vjp(rms_scale, middle, second_gain)
    d_middle_norm, second_part = second_pull(picked[:, width:])
    d_middle = grad_top + d_middle_norm
    all_d_middle = lax.all_gather(d_middle.astype(bf16), "context", axis=0, tiled=True)

    out_rows = jnp.pad(out_weight, ((0, spare * size), (0, 0)))
    my_out = lax.dynamic_slice_in_dim(out_rows, me * share, share, 0)
    d_att = (
        dot(all_d_middle, my_out, NT).astype(bf16).reshape(total, group, size).transpose(1, 0, 2)
    )
    dq, dk, dv, d_scores = attend_back(q, k, v, att, d_att, probs)
    d_qkv = jnp.stack([dq, dk, dv]).transpose(2, 0, 1, 3).reshape(total, 3 * share)
    my_d_middle = lax.dynamic_slice_in_dim(all_d_middle, me * columns, columns, 1)
    qkv_part = dot(normed, d_qkv, TN)
    proj_part = dot(all_att, my_d_middle, TN)
    first_piece = jnp.sum(my_weight.astype(f32) * qkv_part, axis=1) / first_gain
    d_scores, qkv_part = lax.optimization_barrier((d_scores, qkv_part))
    table_part = table_sums(d_scores, ids, buckets).T
    wide_part = jnp.concatenate([qkv_part, proj_part], axis=1).astype(bf16)
    grad_width = 3 * share + columns
    rows_out = width // expert_ranks
    table_out = buckets // expert_ranks
    small = jnp.concatenate(
        [
            first_piece.reshape(expert_ranks, rows_out),
            second_part.reshape(expert_ranks, rows_out),
            table_part.reshape(expert_ranks, table_out * group),
        ],
        axis=1,
    ).astype(bf16)
    small = jnp.pad(small, ((0, 0), (0, grad_width - small.shape[1])))
    wide_part = jnp.concatenate(
        [wide_part.reshape(expert_ranks, rows_out, grad_width), small[:, None, :]], axis=1
    )
    sums = lax.all_to_all(wide_part, "experts", split_axis=0, concat_axis=0, tiled=True)
    d_qkv, _ = lax.optimization_barrier((d_qkv, wide_part))
    outgoing = d_qkv.reshape(ranks, local_rows, 3 * share)
    own = lax.dynamic_update_index_in_dim(
        jnp.zeros_like(outgoing), lax.dynamic_index_in_dim(outgoing, me, 0), me, 0
    )
    for hop in range(1, ranks):
        leaving = lax.dynamic_index_in_dim(outgoing, (me + hop) % ranks, 0)
        met = lax.ppermute(leaving, "context", [(r, (r + hop) % ranks) for r in range(ranks)])
        own = lax.dynamic_update_index_in_dim(own, met, (me - hop) % ranks, 0)
    own = own.reshape(ranks, local_rows, 3, share).transpose(1, 2, 0, 3)
    own = own.reshape(local_rows, 3, ranks * share)[:, :, :width].reshape(local_rows, 3 * width)
    d_first = dot(own, qkv_weight, NT)
    _, first_pull = jax.vjp(lambda values: rms_scale(values, first_gain), features)
    (d_input_norm,) = first_pull(d_first)
    input_grad = (d_middle + d_input_norm)[None]

    sums = jnp.sum(sums.astype(f32), axis=0).astype(bf16)
    full = lax.all_gather(sums, "context", axis=0, tiled=False).astype(f32)
    qkv_grad = full[:, :rows_out, : 3 * share].reshape(ranks, rows_out, 3, share)
    qkv_grad = qkv_grad.transpose(1, 2, 0, 3).reshape(rows_out, 3, ranks * share)
    qkv_grad = qkv_grad[:, :, :width].reshape(rows_out, 3 * width)
    proj_grad = full[:, :rows_out, 3 * share :].transpose(1, 0, 2).reshape(rows_out, width)
    last = full[:, rows_out]
    first_grad = jnp.sum(last[:, :rows_out], axis=0)
    second_grad = jnp.sum(last[:, rows_out : 2 * rows_out], axis=0)
    table_grad = last[:, 2 * rows_out : 2 * rows_out + table_out * group]
    table_grad = table_grad.reshape(ranks, table_out, group).transpose(1, 0, 2)
    table_grad = table_grad.reshape(table_out, ranks * group)[:, :heads]
    return (
        block_output,
        input_grad,
        qkv_grad,
        proj_grad,
        first_grad,
        second_grad,
        table_grad,
        inner_grad,
        down_grad,
    )


def solution(mesh):
    placed = (
        P("experts", "context", None),
        P(),
        P(),
        P(),
        P(),
        P(),
        P("context", None),
        P("experts", "context"),
        P("experts", "context"),
        P("experts", "context"),
        P("experts", None, "context"),
        P("experts", "context", None),
        P("experts", "context", None),
    )
    return jax.shard_map(
        body,
        mesh=mesh,
        in_specs=placed,
        out_specs=(
            P("experts", "context", None),
            P("experts", "context", None),
            P("experts", None),
            P("experts", None),
            P("experts"),
            P("experts"),
            P("experts", None),
            P("experts", None, "context"),
            P("experts", "context", None),
        ),
        check_vma=False,
    )
```
